512 devices in a mesh: ctx: 32 (over y, z_hi), tp: 8 (over x, z_lo), grp: 2 (over core).
Axes of the slice: x: 4, y: 8, z: 8 (z_hi: 4, z_lo: 2; z = z_hi * 2 + z_lo), core: 2. Of those that a mesh axis runs over, the one named last changes fastest.
Arguments:
- queries: bfloat16 [2, 4096, 8192], P('grp', 'ctx', 'tp')
- rotated_new_keys: bfloat16 [2, 4096, 1024], P('grp', 'ctx', 'tp')
- fresh_token_values: bfloat16 [2, 4096, 1024], P('grp', 'ctx', 'tp'), may hold values from -6 to 6
- prefix_cached_keys: bfloat16 [2, 2048, 1024], P('grp', 'ctx', 'tp'), may hold values from -6 to 6
- prefix_cached_values: bfloat16 [2, 2048, 1024], P('grp', 'ctx', 'tp'), may hold values from -6 to 6
- prompt_len: int32 [2], P('grp'), may hold values from 1024 to 4096, as said below
- prefix_len: int32 [2], P('grp'), may hold values from 0 to 2048, as said below
- decode_page_slots: int32 [2, 256], P('grp'), may hold values from 0 to 255, each once within a row
Outputs:
- attended: bfloat16 [2, 4096, 8192], P('grp', 'ctx', 'tp')
- key_pool: bfloat16 [2, 4096, 1024], P('grp', ('ctx', 'tp'))
- value_pool: bfloat16 [2, 4096, 1024], P('grp', ('ctx', 'tp'))
The draws below stay inside these ranges and needn't reach their ends.
Inputs may be any that keep to these rules, and one draw needn't show every extreme that they name: `prompt_len`: one of the two groups has a full prompt. `prefix_len`: one of the two groups has a full cached prefix.
All inputs are finite; a program needn't handle non-finite values.
Results may differ from the reference program's by a relative error of at most 0.01.
Values may be sent and summed in bfloat16 or wider, within the bound.
No kernel may reach another device: no remote copies, remote signals or barrier semaphores. Data moves between devices by JAX's collectives and lax.ppermute only.
A program may use at most 64 MiB of HBM per device.

```python
import math
import jax
import jax.numpy as jnp
from jax import lax

QUERY_HEADS = 64
KEY_VALUE_HEADS = 8
HEAD_SIZE = 128
PAGE_TOKENS = 16
NEW_TOKEN_SLOTS = 4096
CACHED_SLOTS = 2048
NEW_PAGE_COUNT = 256


def shared_keys(key, part):
    return jax.random.normal(key, (2, NEW_TOKEN_SLOTS, KEY_VALUE_HEADS * HEAD_SIZE), jnp.float32)


def draw_rotated_new_keys(key, part):
    base_offset = shared_keys(key, part)
    return base_offset.astype(jnp.bfloat16)


def draw_queries(key, part):
    key = jax.random.fold_in(key, 7)
    key_a = jax.random.fold_in(key, 0)
    drawn = jax.random.normal(key_a, (2, NEW_TOKEN_SLOTS, QUERY_HEADS * HEAD_SIZE), jnp.float32)
    return drawn.astype(jnp.bfloat16)


def draw_prompt_len(key, part):
    key = jax.random.fold_in(key, 11)
    key_a, key_b = jax.random.split(key)
    short = jax.random.randint(key_a, (), NEW_TOKEN_SLOTS // 4, NEW_TOKEN_SLOTS)
    flip = jax.random.randint(key_b, (), 0, 2)
    full = jnp.int32(NEW_TOKEN_SLOTS)
    return jnp.where(flip == 0, jnp.stack([full, short]), jnp.stack([short, full])).astype(jnp.int32)


def draw_prefix_len(key, part):
    key = jax.random.fold_in(key, 29)
    key_a = jax.random.fold_in(key, 0)
    key_c = jax.random.fold_in(key, 2)
    wide = jax.random.randint(key_a, (), 0, 1 << 30)
    short = (wide % CACHED_SLOTS).astype(jnp.int32)
    flip = jax.random.randint(key_c, (), 0, 1 << 20) // 128 % 2
    full = jnp.int32(CACHED_SLOTS)
    return jnp.where(flip == 0, jnp.stack([full, short]), jnp.stack([short, full])).astype(jnp.int32)


def steps_of(rng, dims, cuts, least, high):
    factor_of, own = 1.0, jax.random.fold_in(rng, 6)
    for position, parts in cuts:
        heights = jnp.exp(jax.random.uniform(jax.random.fold_in(own, position), (parts,), jnp.float32, least / len(cuts), high / len(cuts)))
        factor_of = factor_of * jnp.repeat(heights, dims[position] // parts).reshape([-1 if axis == position else 1 for axis in range(len(dims))])
    return factor_of


def gaussian(rng, shape, spread, reach, pieces=(), kind=jnp.bfloat16):
    drawn = spread * jax.random.normal(rng, shape, jnp.float32)
    if pieces:
        drawn = drawn * steps_of(rng, shape, pieces, -0.22, 0.18)
    return jnp.clip(drawn, -reach, reach).astype(kind)


def setup_inputs(seed: int = 0) -> dict:
    arg_keys = jax.random.split(jax.random.key(seed), 9)
    return {
        "queries": draw_queries(jax.random.fold_in(arg_keys[8], 71), 0),
        "rotated_new_keys": draw_rotated_new_keys(jax.random.fold_in(arg_keys[8], 71), 0),
        "fresh_token_values": gaussian(arg_keys[2], (2, NEW_TOKEN_SLOTS, KEY_VALUE_HEADS * HEAD_SIZE), 1.0, 6.0, ((0, 2), (1, 32), (2, 8))),
        "prefix_cached_keys": gaussian(arg_keys[3], (2, CACHED_SLOTS, KEY_VALUE_HEADS * HEAD_SIZE), 1.0, 6.0, ((0, 2), (1, 32), (2, 8))),
        "prefix_cached_values": gaussian(arg_keys[4], (2, CACHED_SLOTS, KEY_VALUE_HEADS * HEAD_SIZE), 1.0, 6.0, ((0, 2), (1, 32), (2, 8))),
        "prompt_len": draw_prompt_len(jax.random.fold_in(arg_keys[8], 71), 0),
        "prefix_len": draw_prefix_len(jax.random.fold_in(arg_keys[8], 71), 0),
        "decode_page_slots": jax.vmap(lambda own: jax.random.permutation(own, NEW_PAGE_COUNT))(jax.random.split(arg_keys[7], 2)).reshape((2, NEW_PAGE_COUNT)).astype(jnp.int32),
    }


def attend_group(group_queries, group_keys, group_values, prefix, length):
    query_per_key_ratio = QUERY_HEADS // KEY_VALUE_HEADS
    scale = HEAD_SIZE ** -0.5
    qblock = math.gcd(NEW_TOKEN_SLOTS, 512)
    nblocks = NEW_TOKEN_SLOTS // qblock
    kidx = jnp.arange(CACHED_SLOTS + NEW_TOKEN_SLOTS, dtype=jnp.int32)
    is_cache = kidx < CACHED_SLOTS
    newpos = kidx - CACHED_SLOTS
    query_head_rows = group_queries.reshape(NEW_TOKEN_SLOTS, KEY_VALUE_HEADS, query_per_key_ratio, HEAD_SIZE).transpose(1, 2, 0, 3)
    key_head_rows = group_keys.reshape(CACHED_SLOTS + NEW_TOKEN_SLOTS, KEY_VALUE_HEADS, HEAD_SIZE).transpose(1, 0, 2)
    value_head_rows = group_values.reshape(CACHED_SLOTS + NEW_TOKEN_SLOTS, KEY_VALUE_HEADS, HEAD_SIZE).transpose(1, 0, 2)

    def one_head(args):
        qh, kh, vh = args
        blocks = qh.reshape(query_per_key_ratio, nblocks, qblock, HEAD_SIZE).transpose(1, 0, 2, 3)

        def one_block(inner):
            index, qb = inner
            qpos = index * qblock + jnp.arange(qblock, dtype=jnp.int32)
            scores = jnp.einsum("gqd,kd->gqk", qb.astype(jnp.float32), kh.astype(jnp.float32)) * scale
            visible = jnp.where(is_cache[None, :], (kidx < prefix)[None, :],
                                (newpos[None, :] < length) & (newpos[None, :] <= qpos[:, None]))
            scores = jnp.where(visible[None], scores, jnp.float32(-1e30))
            top = jnp.max(scores, axis=-1, keepdims=True)
            weights = jnp.where(visible[None], jnp.exp(scores - top), jnp.float32(0.0))
            total = jnp.sum(weights, axis=-1)
            probs = weights.astype(jnp.bfloat16)
            summed = jnp.einsum("gqk,kd->gqd", probs.astype(jnp.float32), vh.astype(jnp.float32))
            return summed / total[..., None]

        result = lax.map(one_block, (jnp.arange(nblocks, dtype=jnp.int32), blocks))
        return result.transpose(1, 0, 2, 3).reshape(query_per_key_ratio, NEW_TOKEN_SLOTS, HEAD_SIZE)

    outs = lax.map(one_head, (query_head_rows, key_head_rows, value_head_rows))
    outs = outs.transpose(2, 0, 1, 3).reshape(NEW_TOKEN_SLOTS, QUERY_HEADS * HEAD_SIZE)
    live_entries = jnp.arange(NEW_TOKEN_SLOTS, dtype=jnp.int32) < length
    return jnp.where(live_entries[:, None], outs, jnp.float32(0.0)).astype(jnp.bfloat16)


def reference(queries, rotated_new_keys, fresh_token_values, prefix_cached_keys, prefix_cached_values, prompt_len, prefix_len, decode_page_slots):
    attended = []
    paged_keys = []
    paged_values = []
    for group_index in range(2):
        k_all = jnp.concatenate([prefix_cached_keys[group_index], rotated_new_keys[group_index]], axis=0)
        v_all = jnp.concatenate([prefix_cached_values[group_index], fresh_token_values[group_index]], axis=0)
        attended.append(attend_group(queries[group_index], k_all, v_all, prefix_len[group_index], prompt_len[group_index]))
        live_entries = (jnp.arange(NEW_TOKEN_SLOTS, dtype=jnp.int32) < prompt_len[group_index])[:, None]
        zero_fill = jnp.zeros((), jnp.bfloat16)
        key_mask = jnp.where(live_entries, rotated_new_keys[group_index], zero_fill).reshape(NEW_PAGE_COUNT, PAGE_TOKENS, KEY_VALUE_HEADS * HEAD_SIZE)
        value_mask = jnp.where(live_entries, fresh_token_values[group_index], zero_fill).reshape(NEW_PAGE_COUNT, PAGE_TOKENS, KEY_VALUE_HEADS * HEAD_SIZE)
        paged_keys.append(jnp.zeros_like(key_mask).at[decode_page_slots[group_index]].set(key_mask).reshape(NEW_PAGE_COUNT * PAGE_TOKENS, KEY_VALUE_HEADS * HEAD_SIZE))
        paged_values.append(jnp.zeros_like(value_mask).at[decode_page_slots[group_index]].set(value_mask).reshape(NEW_PAGE_COUNT * PAGE_TOKENS, KEY_VALUE_HEADS * HEAD_SIZE))
    attended = jnp.stack(attended)
    key_pool = jnp.stack([paged_keys[1], paged_keys[0]])
    value_pool = jnp.stack([paged_values[1], paged_values[0]])
    return attended, key_pool, value_pool
```

```python
import functools
import math

import jax
import jax.numpy as jnp
from jax import lax
from jax.experimental import pallas as pl
from jax.experimental.pallas import tpu as pltpu
from jax.sharding import Mesh, PartitionSpec as P

HEAD = 128
PAGE = 16
HEADS = 8
NEW = 128
OLD = 64
ROWS = 2 * NEW + 2 * OLD
Z, Y = 4, 8
STEP_NEW, STEP_OLD = Z * NEW, Z * OLD
SCALE = 1.0 / math.sqrt(HEAD) * math.log2(math.e)


def shift(value, axes, apart, sizes):
    count = math.prod(sizes)

    def moved(i):
        at, out = [], 0
        for size in reversed(sizes):
            at.append(i % size)
            i //= size
        for place, step, size in zip(reversed(at), apart, sizes):
            out = out * size + (place + step) % size
        return out

    return lax.ppermute(value, axes, [(i, moved(i)) for i in range(count)])


def attend_kernel(scal, q_ref, kv_ref, o_ref, m_ref, acc_ref):
    j = pl.program_id(0)
    ctx, length, prefix = scal[0], scal[1], scal[2]
    y = lax.div(ctx, Z)
    width = STEP_NEW + STEP_OLD
    tile = 256
    heads = tile // NEW

    @pl.when(j == 0)
    def _():
        m_ref[...] = jnp.full(m_ref.shape, -1e30, jnp.float32)
        acc_ref[...] = jnp.zeros(acc_ref.shape, jnp.float32)

    def step(masked):
        k = jnp.concatenate(
            [kv_ref[z, 0:NEW, :] for z in range(Z)]
            + [kv_ref[z, 2 * NEW : 2 * NEW + OLD, :] for z in range(Z)],
            axis=0,
        )
        v = jnp.concatenate(
            [kv_ref[z, NEW : 2 * NEW, :] for z in range(Z)]
            + [kv_ref[z, 2 * NEW + OLD : ROWS, :] for z in range(Z)],
            axis=0,
        )
        v = jnp.concatenate([v, jnp.ones_like(v)], axis=1)
        for t in range(HEADS // heads):
            q = jnp.concatenate(
                [q_ref[:, (t * heads + i) * HEAD : (t * heads + i + 1) * HEAD] for i in range(heads)],
                axis=0,
            )
            s = lax.dot_general(q, k, (((1,), (1,)), ((), ())), preferred_element_type=jnp.float32)
            if masked:
                col = lax.broadcasted_iota(jnp.int32, (tile, width), 1)
                row = lax.broadcasted_iota(jnp.int32, (tile, width), 0) & (NEW - 1)
                new = col < STEP_NEW
                place = jnp.where(new, col + j * STEP_NEW, col - STEP_NEW + j * STEP_OLD)
                limit = jnp.where(new, row + (ctx * NEW + 1), prefix)
                s = jnp.where(place < limit, s, -1e30)
            r = pl.ds(t * tile, tile)
            old = m_ref[r, :]
            top = jnp.maximum(old, jnp.max(s, axis=1, keepdims=True))
            p = jnp.exp2((s - top[:, :1]) * SCALE)
            factor = jnp.exp2((old - top) * SCALE)
            m_ref[r, :] = top
            pv = jnp.dot(p.astype(jnp.bfloat16), v, preferred_element_type=jnp.float32)
            acc_ref[r, :] = acc_ref[r, :] * jnp.concatenate([factor, factor], axis=1) + pv

    live = ctx * NEW < length
    full = (j < y) & ((j + 1) * STEP_OLD <= prefix)
    some = (j <= y) | (j * STEP_OLD < prefix)

    @pl.when(live & full)
    def _():
        step(False)

    @pl.when(live & some & jnp.logical_not(full))
    def _():
        step(True)

    @pl.when(j == pl.num_programs(0) - 1)
    def _():
        row = lax.broadcasted_iota(jnp.int32, (NEW, HEAD), 0) + ctx * NEW
        for h in range(HEADS):
            a = acc_ref[pl.ds(h * NEW, NEW), :]
            o = a[:, :HEAD] / a[:, HEAD:]
            o_ref[:, h * HEAD : (h + 1) * HEAD] = jnp.where(row < length, o, 0.0).astype(jnp.bfloat16)


def attend(scal, q, kv):
    return pl.pallas_call(
        attend_kernel,
        grid_spec=pltpu.PrefetchScalarGridSpec(
            num_scalar_prefetch=1,
            grid=(Y,),
            in_specs=[
                pl.BlockSpec((NEW, HEADS * HEAD), lambda j, s: (0, 0)),
                pl.BlockSpec((Z, ROWS, HEAD), lambda j, s: (j, 0, 0)),
            ],
            out_specs=pl.BlockSpec((NEW, HEADS * HEAD), lambda j, s: (0, 0)),
            scratch_shapes=[
                pltpu.VMEM((HEADS * NEW, HEAD), jnp.float32),
                pltpu.VMEM((HEADS * NEW, 2 * HEAD), jnp.float32),
            ],
        ),
        out_shape=jax.ShapeDtypeStruct((NEW, HEADS * HEAD), jnp.bfloat16),
        compiler_params=pltpu.CompilerParams(vmem_limit_bytes=40 << 20),
        cost_estimate=pl.CostEstimate(
            flops=4 * HEADS * NEW * Y * (STEP_NEW + STEP_OLD) * HEAD,
            bytes_accessed=4 << 20,
            transcendentals=HEADS * NEW * Y * (STEP_NEW + STEP_OLD),
        ),
        name="attend",
    )(scal, q, kv)


PAGES = Z * NEW // PAGE


def place_kernel(scal, slots, kv_ref, o_ref):
    ctx, length = scal[0], scal[1]
    y, z = lax.div(ctx, Z), lax.rem(ctx, Z)
    o_ref[...] = jnp.zeros(o_ref.shape, jnp.bfloat16)
    row = lax.broadcasted_iota(jnp.int32, (PAGE, HEAD), 0)
    for page in range(PAGES):
        slot = slots[y * PAGES + page]
        at = lax.div(slot, 8)
        src, first = page * PAGE // NEW, page * PAGE % NEW

        @pl.when(lax.rem(at, Z) == z)
        def _():
            to = lax.div(at, Z) * 8 + lax.rem(slot, 8)
            keep = row < length - (y * PAGES + page) * PAGE
            for half in range(2):
                rows = kv_ref[src, half * NEW + first : half * NEW + first + PAGE, :]
                rows = jnp.where(keep, rows.astype(jnp.float32), 0.0).astype(jnp.bfloat16)
                o_ref[to, half * PAGE : (half + 1) * PAGE, :] = rows


def place(scal, slots, kv, tps):
    return pl.pallas_call(
        place_kernel,
        grid_spec=pltpu.PrefetchScalarGridSpec(
            num_scalar_prefetch=2,
            grid=(1,),
            in_specs=[pl.BlockSpec((Z, 2 * NEW, HEAD), lambda j, s, t: (0, 0, 0))],
            out_specs=pl.BlockSpec((Y * tps, 2 * PAGE, HEAD), lambda j, s, t: (0, 0, 0)),
        ),
        out_shape=jax.ShapeDtypeStruct((Y * tps, 2 * PAGE, HEAD), jnp.bfloat16),
        compiler_params=pltpu.CompilerParams(vmem_limit_bytes=16 << 20),
        name="place_pages",
    )(scal, slots, kv)


def body(q, new_k, new_v, old_k, old_v, prompt_len, prefix_len, slots):
    ctx = lax.axis_index(("y", "zh")).astype(jnp.int32)
    tp = lax.axis_index(("x", "zl")).astype(jnp.int32)
    tps = lax.axis_size(("x", "zl"))
    scal = jnp.stack([ctx, prompt_len[0], prefix_len[0]])
    slots = slots[0]
    mine = jnp.concatenate([new_k[0], new_v[0], old_k[0], old_v[0]], axis=0)
    column = lax.all_gather(mine, "zh", axis=0)
    everything = lax.all_gather(column, "y", axis=0, tiled=True)

    sent = place(scal, slots, column, tps)
    got = lax.all_to_all(sent, ("y", "x", "zl"), split_axis=0, concat_axis=0, tiled=True)
    page = jnp.sum(jnp.where(slots == ctx * tps + tp, jnp.arange(slots.shape[0], dtype=jnp.int32), 0))
    from_y = lax.div(page, jnp.int32(PAGES))
    got = got.reshape(Y, tps, 2 * PAGE, HEAD)
    got = lax.dynamic_index_in_dim(got, from_y, 0, keepdims=False)
    got = shift(got, "core", (1,), (2,))
    got = got.transpose(1, 0, 2).reshape(2 * PAGE, tps * HEAD)
    out = attend(scal, q[0], everything)
    return out[None], got[None, :PAGE], got[None, PAGE:]


def solution(mesh):
    grid = Mesh(mesh.devices.reshape(Y, Z, 4, 2, 2), ("y", "zh", "x", "zl", "core"))
    ctx, tp = ("y", "zh"), ("x", "zl")
    split = P("core", ctx, tp)
    in_specs = (split, split, split, split, split, P("core"), P("core"), P("core", None))
    out_specs = (split, P("core", ctx + tp, None), P("core", ctx + tp, None))
    return jax.shard_map(body, mesh=grid, in_specs=in_specs, out_specs=out_specs, check_vma=False)
```

```python
import functools
import math

import jax
import jax.numpy as jnp
from jax import lax
from jax.experimental import pallas as pl
from jax.experimental.pallas import tpu as pltpu
from jax.sharding import Mesh, PartitionSpec as P

HEAD = 128
PAGE = 16
HEADS = 8
NEW = 128
OLD = 64
ROWS = 2 * NEW + 2 * OLD
Z, Y = 4, 8
STEP_NEW, STEP_OLD = Z * NEW, Z * OLD
COST = 40
SCALE = 1.0 / math.sqrt(HEAD) * math.log2(math.e)


def shift(value, axes, apart, sizes):
    count = math.prod(sizes)

    def moved(i):
        at, out = [], 0
        for size in reversed(sizes):
            at.append(i % size)
            i //= size
        for place, step, size in zip(reversed(at), apart, sizes):
            out = out * size + (place + step) % size
        return out

    return lax.ppermute(value, axes, [(i, moved(i)) for i in range(count)])


def attend_kernel(scal, q_ref, *refs, apart, first, last):
    count = len(apart)
    blocks, refs = refs[:count], refs[count:]
    if not first:
        m_ref, acc_ref, *refs = refs
    o_ref = None
    if last:
        o_ref, *refs = refs
    elif first:
        m_ref, acc_ref, *refs = refs
    else:
        m_ref, acc_ref, *refs = refs
    held, arrived = refs
    copies = [pltpu.make_async_copy(blocks[i], held.at[i], arrived.at[i]) for i in range(count)]
    for copy in copies:
        copy.start()
    if first:
        m_ref[...] = jnp.full(m_ref.shape, -1e30, jnp.float32)
        acc_ref[...] = jnp.zeros(acc_ref.shape, jnp.float32)
    ctx, length, prefix = scal[0], scal[1], scal[2]
    y = lax.div(ctx, Z)
    live = ctx * NEW < length
    tile = 256
    heads = tile // NEW

    def step(i, j, masked, with_new=True):
        new_keys = STEP_NEW if with_new else 0
        width = new_keys + STEP_OLD
        k = [held[i, z, 0:NEW, :] for z in range(Z)] if with_new else []
        k += [held[i, z, 2 * NEW : 2 * NEW + OLD, :] for z in range(Z)]
        v = [held[i, z, NEW : 2 * NEW, :] for z in range(Z)] if with_new else []
        v += [held[i, z, 2 * NEW + OLD : ROWS, :] for z in range(Z)]
        k, v = jnp.concatenate(k, axis=0), jnp.concatenate(v, axis=0)
        v = jnp.concatenate([v, jnp.ones_like(v)], axis=1)

        def scores(t):
            q = jnp.concatenate(
                [q_ref[:, (t * heads + n) * HEAD : (t * heads + n + 1) * HEAD] for n in range(heads)],
                axis=0,
            )
            s = lax.dot_general(q, k, (((1,), (1,)), ((), ())), preferred_element_type=jnp.float32)
            if masked:
                col = lax.broadcasted_iota(jnp.int32, (tile, width), 1)
                row = lax.broadcasted_iota(jnp.int32, (tile, width), 0) & (NEW - 1)
                new = col < new_keys
                place = jnp.where(new, col + j * STEP_NEW, col - new_keys + j * STEP_OLD)
                limit = jnp.where(new, row + (ctx * NEW + 1), prefix)
                s = jnp.where(place < limit, s, -1e30)
            return s

        s = scores(0)
        for t in range(HEADS // heads):
            ahead = scores(t + 1) if t + 1 < HEADS // heads else None
            r = pl.ds(t * tile, tile)
            old = m_ref[r, :]
            top = jnp.maximum(old, jnp.max(s, axis=1, keepdims=True))
            p = jnp.exp2((s - top[:, :1]) * SCALE)
            factor = jnp.exp2((old - top) * SCALE)
            m_ref[r, :] = top
            pv = jnp.dot(p.astype(jnp.bfloat16), v, preferred_element_type=jnp.float32)
            acc_ref[r, :] = acc_ref[r, :] * jnp.concatenate([factor, factor], axis=1) + pv
            s = ahead

    for i, far in enumerate(apart):
        copies[i].wait()
        j = lax.rem(y + far + Y, Y)
        old_full = (j + 1) * STEP_OLD <= prefix
        old_some = j * STEP_OLD < prefix
        if far == 0:
            pl.when(live)(functools.partial(step, i, j, True))
        else:
            pl.when(live & (j < y) & old_full)(functools.partial(step, i, j, False))
            pl.when(live & (j < y) & jnp.logical_not(old_full))(functools.partial(step, i, j, True))
            pl.when(live & (j > y) & old_some)(functools.partial(step, i, j, True, False))

    if last:
        row = lax.broadcasted_iota(jnp.int32, (NEW, HEAD), 0) + ctx * NEW
        for h in range(HEADS):
            a = acc_ref[pl.ds(h * NEW, NEW), :]
            o = a[:, :HEAD] / a[:, HEAD:]
            o_ref[:, h * HEAD : (h + 1) * HEAD] = jnp.where(row < length, o, 0.0).astype(jnp.bfloat16)


def attend(scal, q, blocks, apart, state=None, last=False):
    whole = pl.BlockSpec(memory_space=pltpu.VMEM)
    saved = (
        jax.ShapeDtypeStruct((HEADS * NEW, HEAD), jnp.float32),
        jax.ShapeDtypeStruct((HEADS * NEW, 2 * HEAD), jnp.float32),
    )
    first, count = state is None, len(apart)
    keys = count * (STEP_NEW + STEP_OLD)
    return pl.pallas_call(
        functools.partial(attend_kernel, apart=apart, first=first, last=last),
        in_specs=[pl.BlockSpec(memory_space=pltpu.SMEM), whole]
        + [pl.BlockSpec(memory_space=pl.ANY)] * count
        + ([] if first else [whole] * 2),
        out_specs=whole if last else (whole, whole),
        out_shape=jax.ShapeDtypeStruct((NEW, HEADS * HEAD), jnp.bfloat16) if last else saved,
        input_output_aliases={} if first or last else {2 + count: 0, 3 + count: 1},
        scratch_shapes=[
            pltpu.VMEM((count, Z, ROWS, HEAD), jnp.bfloat16),
            pltpu.SemaphoreType.DMA((count,)),
        ],
        compiler_params=pltpu.CompilerParams(vmem_limit_bytes=32 << 20),
        cost_estimate=pl.CostEstimate(
            flops=COST * HEADS * NEW * keys * HEAD,
            bytes_accessed=count * Z * ROWS * HEAD * 2,
            transcendentals=HEADS * NEW * keys,
        ),
        name="attend_blocks",
    )(scal, q, *blocks, *(() if first else state))


PAGES = Z * NEW // PAGE


def pick_kernel(scal, pages, *refs):
    blocks, (o_ref, held, arrived) = refs[:Y], refs[Y:]
    y, length = lax.div(scal[0], Z), scal[1]
    count = held.shape[0]
    for k in range(count):
        page = pages[k]
        away = lax.rem(lax.div(page, PAGES) - y + Y, Y)
        inside = lax.rem(page, PAGES)
        z = lax.div(inside, NEW // PAGE)
        first = pl.multiple_of(lax.rem(inside, NEW // PAGE) * PAGE, PAGE)
        for d in range(Y):

            @pl.when(away == d)
            def _():
                for half in range(2):
                    pltpu.make_async_copy(
                        blocks[d].at[z, pl.ds(half * NEW + first, PAGE)],
                        held.at[k, pl.ds(half * PAGE, PAGE)],
                        arrived.at[k, half],
                    ).start()

    row = lax.broadcasted_iota(jnp.int32, (PAGE, HEAD), 0)
    for k in range(count):
        keep = row < length - pages[k] * PAGE
        for half in range(2):
            rows = pl.ds(half * PAGE, PAGE)
            pltpu.make_async_copy(
                blocks[0].at[0, pl.ds(0, PAGE)], held.at[k, rows], arrived.at[k, half]
            ).wait()
            page = jnp.where(keep, held[k, rows, :].astype(jnp.float32), 0.0).astype(jnp.bfloat16)
            for core in range(2):
                o_ref[k, core, rows, :] = page


def pick(scal, pages, blocks):
    count = pages.shape[0]
    small = pl.BlockSpec(memory_space=pltpu.SMEM)
    return pl.pallas_call(
        pick_kernel,
        in_specs=[small, small] + [pl.BlockSpec(memory_space=pl.ANY)] * Y,
        out_specs=pl.BlockSpec(memory_space=pltpu.VMEM),
        out_shape=jax.ShapeDtypeStruct((count, 2, 2 * PAGE, HEAD), jnp.bfloat16),
        scratch_shapes=[
            pltpu.VMEM((count, 2 * PAGE, HEAD), jnp.bfloat16),
            pltpu.SemaphoreType.DMA((count, 2)),
        ],
        name="pick_pages",
    )(scal, pages, *blocks)


def assemble_kernel(core, got_ref, k_ref, v_ref):
    other = 1 - core[0]
    for t in range(got_ref.shape[0]):
        for half, out in enumerate((k_ref, v_ref)):
            out[0, :, t * HEAD : (t + 1) * HEAD] = got_ref[t, other, half * PAGE : (half + 1) * PAGE, :]


def assemble(core, got):
    tps = got.shape[0]
    whole = pl.BlockSpec(memory_space=pltpu.VMEM)
    return pl.pallas_call(
        assemble_kernel,
        in_specs=[pl.BlockSpec(memory_space=pltpu.SMEM), whole],
        out_specs=(whole, whole),
        out_shape=(jax.ShapeDtypeStruct((1, PAGE, tps * HEAD), jnp.bfloat16),) * 2,
        name="assemble_pages",
    )(core, got)


def farthest(right, left):
    core = lax.axis_index("core")
    pairs = []
    for i in range(2 * Y):
        y, c = i // 2, i % 2
        pairs.append((i, (y + (1 if c == 0 else -1)) % Y * 2 + c))
    return lax.ppermute(jnp.where(core == 0, right, left), ("y", "core"), pairs)


def body(q, new_k, new_v, old_k, old_v, prompt_len, prefix_len, slots):
    ctx = lax.axis_index(("y", "zh")).astype(jnp.int32)
    core = lax.axis_index("core").astype(jnp.int32)
    tps = lax.axis_size(("x", "zl"))
    scal = jnp.stack([ctx, prompt_len[0], prefix_len[0]])
    mine = jnp.concatenate([new_k[0], new_v[0], old_k[0], old_v[0]], axis=0)
    column = lax.all_gather(mine, "zh", axis=0)
    right, left = [column], [column]
    for _ in range(3):
        right.append(shift(right[-1], ("y",), (1,), (Y,)))
        left.append(shift(left[-1], ("y",), (-1,), (Y,)))
    far = farthest(right[3], left[3])

    slots_here = ctx * tps + jnp.arange(tps, dtype=jnp.int32)
    page_ids = jnp.arange(slots.shape[1], dtype=jnp.int32)
    pages = jnp.sum(jnp.where(slots[0][None, :] == slots_here[:, None], page_ids[None, :], 0), axis=1)
    by_distance = [column, left[1], left[2], left[3], far, right[3], right[2], right[1]]
    sent = pick(scal, pages, by_distance).reshape(2 * tps, 2 * PAGE, HEAD)
    got = lax.all_to_all(sent, ("x", "zl", "core"), split_axis=0, concat_axis=0, tiled=True)
    pools = assemble(core[None], got.reshape(tps, 2, 2 * PAGE, HEAD))

    state = attend(scal, q[0], [column], (0,))
    for away in (1, 2, 3):
        state = attend(scal, q[0], [right[away], left[away]], (-away, away), state)
    out = attend(scal, q[0], [far], (4,), state, last=True)
    return (out[None], *pools)


def solution(mesh):
    grid = Mesh(mesh.devices.reshape(Y, Z, 4, 2, 2), ("y", "zh", "x", "zl", "core"))
    ctx, tp = ("y", "zh"), ("x", "zl")
    split = P("core", ctx, tp)
    in_specs = (split, split, split, split, split, P("core"), P("core"), P("core", None))
    out_specs = (split, P("core", ctx + tp, None), P("core", ctx + tp, None))
    return jax.shard_map(body, mesh=grid, in_specs=in_specs, out_specs=out_specs, check_vma=False)
```

```python
import functools
import math

import jax
import jax.numpy as jnp
from jax import lax
from jax.experimental import pallas as pl
from jax.experimental.pallas import tpu as pltpu
from jax.sharding import Mesh, PartitionSpec as P

HEAD = 128
PAGE = 16
HEADS = 8
NEW = 128
OLD = 64
ROWS = 2 * NEW + 2 * OLD
Z, Y = 4, 8
STEP_NEW, STEP_OLD = Z * NEW, Z * OLD
COST = 40
SCALE = 1.0 / math.sqrt(HEAD) * math.log2(math.e)


def shift(value, axes, apart, sizes):
    count = math.prod(sizes)

    def moved(i):
        at, out = [], 0
        for size in reversed(sizes):
            at.append(i % size)
            i //= size
        for place, step, size in zip(reversed(at), apart, sizes):
            out = out * size + (place + step) % size
        return out

    return lax.ppermute(value, axes, [(i, moved(i)) for i in range(count)])


def attend_kernel(scal, q_ref, *refs, apart, first, last):
    count = len(apart)
    blocks, refs = refs[:count], refs[count:]
    if not first:
        m_ref, acc_ref, *refs = refs
    if last:
        (o_ref,) = refs
    else:
        m_ref, acc_ref = refs
    if first:
        m_ref[...] = jnp.full(m_ref.shape, -1e30, jnp.float32)
        acc_ref[...] = jnp.zeros(acc_ref.shape, jnp.float32)
    ctx, length, prefix = scal[0], scal[1], scal[2]
    y = lax.div(ctx, Z)
    live = ctx * NEW < length
    tile = 256
    heads = tile // NEW

    def step(i, j, masked, with_new=True):
        new_keys = STEP_NEW if with_new else 0
        width = new_keys + STEP_OLD
        k = [blocks[i][z, 0:NEW, :] for z in range(Z)] if with_new else []
        k += [blocks[i][z, 2 * NEW : 2 * NEW + OLD, :] for z in range(Z)]
        v = [blocks[i][z, NEW : 2 * NEW, :] for z in range(Z)] if with_new else []
        v += [blocks[i][z, 2 * NEW + OLD : ROWS, :] for z in range(Z)]
        k, v = jnp.concatenate(k, axis=0), jnp.concatenate(v, axis=0)
        v = jnp.concatenate([v, jnp.ones_like(v)], axis=1)

        def scores(t):
            q = jnp.concatenate(
                [q_ref[:, (t * heads + n) * HEAD : (t * heads + n + 1) * HEAD] for n in range(heads)],
                axis=0,
            )
            s = lax.dot_general(q, k, (((1,), (1,)), ((), ())), preferred_element_type=jnp.float32)
            if masked:
                col = lax.broadcasted_iota(jnp.int32, (tile, width), 1)
                row = lax.broadcasted_iota(jnp.int32, (tile, width), 0) & (NEW - 1)
                new = col < new_keys
                place = jnp.where(new, col + j * STEP_NEW, col - new_keys + j * STEP_OLD)
                limit = jnp.where(new, row + (ctx * NEW + 1), prefix)
                s = jnp.where(place < limit, s, -1e30)
            return s

        s = scores(0)
        for t in range(HEADS // heads):
            ahead = scores(t + 1) if t + 1 < HEADS // heads else None
            r = pl.ds(t * tile, tile)
            old = m_ref[r, :]
            top = jnp.maximum(old, jnp.max(s, axis=1, keepdims=True))
            p = jnp.exp2((s - top[:, :1]) * SCALE)
            factor = jnp.exp2((old - top) * SCALE)
            m_ref[r, :] = top
            pv = jnp.dot(p.astype(jnp.bfloat16), v, preferred_element_type=jnp.float32)
            acc_ref[r, :] = acc_ref[r, :] * jnp.concatenate([factor, factor], axis=1) + pv
            s = ahead

    for i, far in enumerate(apart):
        j = lax.rem(y + far + Y, Y)
        old_full = (j + 1) * STEP_OLD <= prefix
        old_some = j * STEP_OLD < prefix
        if far == 0:
            pl.when(live)(functools.partial(step, i, j, True))
        else:
            pl.when(live & (j < y) & old_full)(functools.partial(step, i, j, False))
            pl.when(live & (j < y) & jnp.logical_not(old_full))(functools.partial(step, i, j, True))
            pl.when(live & (j > y) & old_some)(functools.partial(step, i, j, True, False))

    if last:
        row = lax.broadcasted_iota(jnp.int32, (NEW, HEAD), 0) + ctx * NEW
        for h in range(HEADS):
            a = acc_ref[pl.ds(h * NEW, NEW), :]
            o = a[:, :HEAD] / a[:, HEAD:]
            o_ref[:, h * HEAD : (h + 1) * HEAD] = jnp.where(row < length, o, 0.0).astype(jnp.bfloat16)


def attend(scal, q, blocks, apart, state=None, last=False):
    whole = pl.BlockSpec(memory_space=pltpu.VMEM)
    saved = (
        jax.ShapeDtypeStruct((HEADS * NEW, HEAD), jnp.float32),
        jax.ShapeDtypeStruct((HEADS * NEW, 2 * HEAD), jnp.float32),
    )
    first, count = state is None, len(apart)
    keys = count * (STEP_NEW + STEP_OLD)
    return pl.pallas_call(
        functools.partial(attend_kernel, apart=apart, first=first, last=last),
        in_specs=[pl.BlockSpec(memory_space=pltpu.SMEM), whole]
        + [whole] * count
        + ([] if first else [whole] * 2),
        out_specs=whole if last else (whole, whole),
        out_shape=jax.ShapeDtypeStruct((NEW, HEADS * HEAD), jnp.bfloat16) if last else saved,
        input_output_aliases={} if first or last else {2 + count: 0, 3 + count: 1},
        compiler_params=pltpu.CompilerParams(vmem_limit_bytes=24 << 20),
        cost_estimate=pl.CostEstimate(
            flops=COST * HEADS * NEW * keys * HEAD,
            bytes_accessed=count * Z * ROWS * HEAD * 2,
            transcendentals=HEADS * NEW * keys,
        ),
        name="attend_blocks",
    )(scal, q, *blocks, *(() if first else state))


PAGES = Z * NEW // PAGE


def pick_kernel(scal, pages, *refs):
    blocks, o_ref = refs[:Y], refs[Y]
    y, length = lax.div(scal[0], Z), scal[1]
    row = lax.broadcasted_iota(jnp.int32, (PAGE, HEAD), 0)
    for k in range(o_ref.shape[0]):
        page = pages[k]
        away = lax.rem(lax.div(page, PAGES) - y + Y, Y)
        inside = lax.rem(page, PAGES)
        z = lax.div(inside, NEW // PAGE)
        first = pl.multiple_of(lax.rem(inside, NEW // PAGE) * PAGE, PAGE)
        keep = row < length - page * PAGE
        for d in range(Y):

            @pl.when(away == d)
            def _():
                for half in range(2):
                    rows = blocks[d][z, pl.ds(half * NEW + first, PAGE), :]
                    rows = jnp.where(keep, rows.astype(jnp.float32), 0.0).astype(jnp.bfloat16)
                    for core in range(2):
                        o_ref[k, core, half * PAGE : (half + 1) * PAGE, :] = rows


def pick(scal, pages, blocks):
    count = pages.shape[0]
    small, whole = pl.BlockSpec(memory_space=pltpu.SMEM), pl.BlockSpec(memory_space=pltpu.VMEM)
    return pl.pallas_call(
        pick_kernel,
        in_specs=[small, small] + [whole] * Y,
        out_specs=whole,
        out_shape=jax.ShapeDtypeStruct((count, 2, 2 * PAGE, HEAD), jnp.bfloat16),
        compiler_params=pltpu.CompilerParams(vmem_limit_bytes=8 << 20),
        name="pick_pages",
    )(scal, pages, *blocks)


def assemble_kernel(core, got_ref, k_ref, v_ref):
    other = 1 - core[0]
    for t in range(got_ref.shape[0]):
        for half, out in enumerate((k_ref, v_ref)):
            out[0, :, t * HEAD : (t + 1) * HEAD] = got_ref[t, other, half * PAGE : (half + 1) * PAGE, :]


def assemble(core, got):
    tps = got.shape[0]
    whole = pl.BlockSpec(memory_space=pltpu.VMEM)
    return pl.pallas_call(
        assemble_kernel,
        in_specs=[pl.BlockSpec(memory_space=pltpu.SMEM), whole],
        out_specs=(whole, whole),
        out_shape=(jax.ShapeDtypeStruct((1, PAGE, tps * HEAD), jnp.bfloat16),) * 2,
        compiler_params=pltpu.CompilerParams(vmem_limit_bytes=8 << 20),
        name="assemble_pages",
    )(core, got)


def body(q, new_k, new_v, old_k, old_v, prompt_len, prefix_len, slots):
    ctx = lax.axis_index(("y", "zh")).astype(jnp.int32)
    core = lax.axis_index("core").astype(jnp.int32)
    tps = lax.axis_size(("x", "zl"))
    scal = jnp.stack([ctx, prompt_len[0], prefix_len[0]])
    mine = jnp.concatenate([new_k[0], new_v[0], old_k[0], old_v[0]], axis=0)
    column = lax.all_gather(mine, "zh", axis=0)
    a, b = [column], [column]
    for _ in range(3):
        a.append(shift(a[-1], ("y",), (1,), (Y,)))
        b.append(shift(b[-1], ("y",), (-1,), (Y,)))
    far = shift(a[3], ("y",), (1,), (Y,))

    slots_here = ctx * tps + jnp.arange(tps, dtype=jnp.int32)
    page_ids = jnp.arange(slots.shape[1], dtype=jnp.int32)
    pages = jnp.sum(jnp.where(slots[0][None, :] == slots_here[:, None], page_ids[None, :], 0), axis=1)
    by_distance = [column, b[1], b[2], b[3], far, a[3], a[2], a[1]]
    sent = pick(scal, pages, by_distance).reshape(2 * tps, 2 * PAGE, HEAD)
    got = lax.all_to_all(sent, ("x", "zl", "core"), split_axis=0, concat_axis=0, tiled=True)
    pools = assemble(core[None], got.reshape(tps, 2, 2 * PAGE, HEAD))

    state = attend(scal, q[0], [column], (0,))
    for away in (1, 2, 3):
        state = attend(scal, q[0], [a[away], b[away]], (-away, away), state)
    out = attend(scal, q[0], [far], (4,), state, last=True)
    return (out[None], *pools)


def solution(mesh):
    grid = Mesh(mesh.devices.reshape(Y, Z, 4, 2, 2), ("y", "zh", "x", "zl", "core"))
    ctx, tp = ("y", "zh"), ("x", "zl")
    split = P("core", ctx, tp)
    in_specs = (split, split, split, split, split, P("core"), P("core"), P("core", None))
    out_specs = (split, P("core", ctx + tp, None), P("core", ctx + tp, None))
    return jax.shard_map(body, mesh=grid, in_specs=in_specs, out_specs=out_specs, check_vma=False)
```

```python
import functools
import math

import jax
import jax.numpy as jnp
from jax import lax
from jax.experimental import pallas as pl
from jax.experimental.pallas import tpu as pltpu
from jax.sharding import Mesh, PartitionSpec as P

HEAD = 128
PAGE = 16
HEADS = 8
NEW = 128
OLD = 64
ROWS = 2 * NEW + 2 * OLD
Z, Y = 4, 8
STEP_NEW, STEP_OLD = Z * NEW, Z * OLD
COST = 40
SCALE = 1.0 / math.sqrt(HEAD) * math.log2(math.e)


def shift(value, axes, apart, sizes):
    count = math.prod(sizes)

    def moved(i):
        at, out = [], 0
        for size in reversed(sizes):
            at.append(i % size)
            i //= size
        for place, step, size in zip(reversed(at), apart, sizes):
            out = out * size + (place + step) % size
        return out

    return lax.ppermute(value, axes, [(i, moved(i)) for i in range(count)])


def attend_kernel(scal, q_ref, *refs, apart, first, last):
    count = len(apart)
    blocks, refs = refs[:count], refs[count:]
    if not first:
        m_ref, acc_ref, *refs = refs
    if last:
        (o_ref,) = refs
    else:
        m_ref, acc_ref = refs
    if first:
        m_ref[...] = jnp.full(m_ref.shape, -1e30, jnp.float32)
        acc_ref[...] = jnp.zeros(acc_ref.shape, jnp.float32)
    ctx, length, prefix = scal[0], scal[1], scal[2]
    y = lax.div(ctx, Z)
    live = ctx * NEW < length
    tile = 256
    heads = tile // NEW

    def step(i, j, masked, with_new=True):
        new_keys = STEP_NEW if with_new else 0
        width = new_keys + STEP_OLD
        k = [blocks[i][z, 0:NEW, :] for z in range(Z)] if with_new else []
        k += [blocks[i][z, 2 * NEW : 2 * NEW + OLD, :] for z in range(Z)]
        v = [blocks[i][z, NEW : 2 * NEW, :] for z in range(Z)] if with_new else []
        v += [blocks[i][z, 2 * NEW + OLD : ROWS, :] for z in range(Z)]
        k, v = jnp.concatenate(k, axis=0), jnp.concatenate(v, axis=0)
        v = jnp.concatenate([v, jnp.ones_like(v)], axis=1)

        def scores(t):
            q = jnp.concatenate(
                [q_ref[:, (t * heads + n) * HEAD : (t * heads + n + 1) * HEAD] for n in range(heads)],
                axis=0,
            )
            s = lax.dot_general(q, k, (((1,), (1,)), ((), ())), preferred_element_type=jnp.float32)
            if masked:
                col = lax.broadcasted_iota(jnp.int32, (tile, width), 1)
                row = lax.broadcasted_iota(jnp.int32, (tile, width), 0) & (NEW - 1)
                new = col < new_keys
                place = jnp.where(new, col + j * STEP_NEW, col - new_keys + j * STEP_OLD)
                limit = jnp.where(new, row + (ctx * NEW + 1), prefix)
                s = jnp.where(place < limit, s, -1e30)
            return s

        s = scores(0)
        for t in range(HEADS // heads):
            ahead = scores(t + 1) if t + 1 < HEADS // heads else None
            r = pl.ds(t * tile, tile)
            old = m_ref[r, :]
            top = jnp.maximum(old, jnp.max(s, axis=1, keepdims=True))
            p = jnp.exp2((s - top[:, :1]) * SCALE)
            factor = jnp.exp2((old - top) * SCALE)
            m_ref[r, :] = top
            pv = jnp.dot(p.astype(jnp.bfloat16), v, preferred_element_type=jnp.float32)
            acc_ref[r, :] = acc_ref[r, :] * jnp.concatenate([factor, factor], axis=1) + pv
            s = ahead

    for i, far in enumerate(apart):
        j = lax.rem(y + far + Y, Y)
        old_full = (j + 1) * STEP_OLD <= prefix
        old_some = j * STEP_OLD < prefix
        if far == 0:
            pl.when(live)(functools.partial(step, i, j, True))
        else:
            pl.when(live & (j < y) & old_full)(functools.partial(step, i, j, False))
            pl.when(live & (j < y) & jnp.logical_not(old_full))(functools.partial(step, i, j, True))
            pl.when(live & (j > y) & old_some)(functools.partial(step, i, j, True, False))

    if last:
        row = lax.broadcasted_iota(jnp.int32, (NEW, HEAD), 0) + ctx * NEW
        for h in range(HEADS):
            a = acc_ref[pl.ds(h * NEW, NEW), :]
            o = a[:, :HEAD] / a[:, HEAD:]
            o_ref[:, h * HEAD : (h + 1) * HEAD] = jnp.where(row < length, o, 0.0).astype(jnp.bfloat16)


def attend(scal, q, blocks, apart, state=None, last=False):
    whole = pl.BlockSpec(memory_space=pltpu.VMEM)
    saved = (
        jax.ShapeDtypeStruct((HEADS * NEW, HEAD), jnp.float32),
        jax.ShapeDtypeStruct((HEADS * NEW, 2 * HEAD), jnp.float32),
    )
    first, count = state is None, len(apart)
    keys = count * (STEP_NEW + STEP_OLD)
    return pl.pallas_call(
        functools.partial(attend_kernel, apart=apart, first=first, last=last),
        in_specs=[pl.BlockSpec(memory_space=pltpu.SMEM), whole]
        + [whole] * count
        + ([] if first else [whole] * 2),
        out_specs=whole if last else (whole, whole),
        out_shape=jax.ShapeDtypeStruct((NEW, HEADS * HEAD), jnp.bfloat16) if last else saved,
        input_output_aliases={} if first or last else {2 + count: 0, 3 + count: 1},
        compiler_params=pltpu.CompilerParams(vmem_limit_bytes=24 << 20),
        cost_estimate=pl.CostEstimate(
            flops=COST * HEADS * NEW * keys * HEAD,
            bytes_accessed=count * Z * ROWS * HEAD * 2,
            transcendentals=HEADS * NEW * keys,
        ),
        name="attend_blocks",
    )(scal, q, *blocks, *(() if first else state))


PAGES = Z * NEW // PAGE


def pick_kernel(scal, pages, *refs):
    blocks, o_ref = refs[:Y], refs[Y]
    y, length = lax.div(scal[0], Z), scal[1]
    row = lax.broadcasted_iota(jnp.int32, (PAGE, HEAD), 0)
    for k in range(o_ref.shape[0]):
        page = pages[k]
        away = lax.rem(lax.div(page, PAGES) - y + Y, Y)
        inside = lax.rem(page, PAGES)
        z = lax.div(inside, NEW // PAGE)
        first = pl.multiple_of(lax.rem(inside, NEW // PAGE) * PAGE, PAGE)
        keep = row < length - page * PAGE
        for half in range(2):
            rows = blocks[0][z, pl.ds(half * NEW + first, PAGE), :]
            for d in range(1, Y):
                rows = jnp.where(away == d, blocks[d][z, pl.ds(half * NEW + first, PAGE), :], rows)
            rows = jnp.where(keep, rows.astype(jnp.float32), 0.0).astype(jnp.bfloat16)
            for core in range(2):
                o_ref[k, core, half * PAGE : (half + 1) * PAGE, :] = rows


def pick(scal, pages, blocks):
    count = pages.shape[0]
    small, whole = pl.BlockSpec(memory_space=pltpu.SMEM), pl.BlockSpec(memory_space=pltpu.VMEM)
    return pl.pallas_call(
        pick_kernel,
        in_specs=[small, small] + [whole] * Y,
        out_specs=whole,
        out_shape=jax.ShapeDtypeStruct((count, 2, 2 * PAGE, HEAD), jnp.bfloat16),
        compiler_params=pltpu.CompilerParams(vmem_limit_bytes=8 << 20),
        name="pick_pages",
    )(scal, pages, *blocks)


def assemble_kernel(core, got_ref, k_ref, v_ref):
    other = 1 - core[0]
    for t in range(got_ref.shape[0]):
        for half, out in enumerate((k_ref, v_ref)):
            out[0, :, t * HEAD : (t + 1) * HEAD] = got_ref[t, other, half * PAGE : (half + 1) * PAGE, :]


def assemble(core, got):
    tps = got.shape[0]
    whole = pl.BlockSpec(memory_space=pltpu.VMEM)
    return pl.pallas_call(
        assemble_kernel,
        in_specs=[pl.BlockSpec(memory_space=pltpu.SMEM), whole],
        out_specs=(whole, whole),
        out_shape=(jax.ShapeDtypeStruct((1, PAGE, tps * HEAD), jnp.bfloat16),) * 2,
        compiler_params=pltpu.CompilerParams(vmem_limit_bytes=8 << 20),
        name="assemble_pages",
    )(core, got)


def body(q, new_k, new_v, old_k, old_v, prompt_len, prefix_len, slots):
    ctx = lax.axis_index(("y", "zh")).astype(jnp.int32)
    core = lax.axis_index("core").astype(jnp.int32)
    tps = lax.axis_size(("x", "zl"))
    scal = jnp.stack([ctx, prompt_len[0], prefix_len[0]])
    mine = jnp.concatenate([new_k[0], new_v[0], old_k[0], old_v[0]], axis=0)
    column = lax.all_gather(mine, "zh", axis=0)
    a, b = [column], [column]
    for _ in range(3):
        a.append(shift(a[-1], ("y",), (-1,), (Y,)))
        b.append(shift(b[-1], ("y",), (1,), (Y,)))
    far = shift(a[3], ("y",), (-1,), (Y,))

    slots_here = ctx * tps + jnp.arange(tps, dtype=jnp.int32)
    page_ids = jnp.arange(slots.shape[1], dtype=jnp.int32)
    pages = jnp.sum(jnp.where(slots[0][None, :] == slots_here[:, None], page_ids[None, :], 0), axis=1)
    by_distance = [column, a[1], a[2], a[3], far, b[3], b[2], b[1]]
    sent = pick(scal, pages, by_distance).reshape(2 * tps, 2 * PAGE, HEAD)
    got = lax.all_to_all(sent, ("x", "zl", "core"), split_axis=0, concat_axis=0, tiled=True)
    pools = assemble(core[None], got.reshape(tps, 2, 2 * PAGE, HEAD))

    state = attend(scal, q[0], [column], (0,))
    for away in (1, 2, 3):
        state = attend(scal, q[0], [a[away], b[away]], (away, -away), state)
    out = attend(scal, q[0], [far], (4,), state, last=True)
    return (out[None], *pools)


def solution(mesh):
    grid = Mesh(mesh.devices.reshape(Y, Z, 4, 2, 2), ("y", "zh", "x", "zl", "core"))
    ctx, tp = ("y", "zh"), ("x", "zl")
    split = P("core", ctx, tp)
    in_specs = (split, split, split, split, split, P("core"), P("core"), P("core", None))
    out_specs = (split, P("core", ctx + tp, None), P("core", ctx + tp, None))
    return jax.shard_map(body, mesh=grid, in_specs=in_specs, out_specs=out_specs, check_vma=False)
```

```python
import functools
import math

import jax
import jax.numpy as jnp
from jax import lax
from jax.experimental import pallas as pl
from jax.experimental.pallas import tpu as pltpu
from jax.sharding import Mesh, PartitionSpec as P

HEAD = 128
PAGE = 16
HEADS = 8
NEW = 128
OLD = 64
ROWS = 2 * NEW + 2 * OLD
Z, Y = 4, 8
STEP_NEW, STEP_OLD = Z * NEW, Z * OLD
COST = 40
SCALE = 1.0 / math.sqrt(HEAD) * math.log2(math.e)


def shift(value, axes, apart, sizes):
    count = math.prod(sizes)

    def moved(i):
        at, out = [], 0
        for size in reversed(sizes):
            at.append(i % size)
            i //= size
        for place, step, size in zip(reversed(at), apart, sizes):
            out = out * size + (place + step) % size
        return out

    return lax.ppermute(value, axes, [(i, moved(i)) for i in range(count)])


def attend_kernel(scal, q_ref, *refs, apart, first, last):
    split = last
    count = len(apart) + split
    blocks, refs = refs[:count], refs[count:]
    if not first:
        m_ref, acc_ref, *refs = refs
    if last:
        (o_ref,) = refs
    else:
        m_ref, acc_ref = refs
    if first:
        m_ref[...] = jnp.full(m_ref.shape, -1e30, jnp.float32)
        acc_ref[...] = jnp.zeros(acc_ref.shape, jnp.float32)
    ctx, length, prefix = scal[0], scal[1], scal[2]
    y = lax.div(ctx, Z)
    live = ctx * NEW < length
    tile = 256
    heads = tile // NEW

    def step(i, j, masked, with_new=True):
        new_ref, old_ref = blocks[i], blocks[-1] if split else blocks[i]
        at = 0 if split else 2 * NEW
        new_keys = STEP_NEW if with_new else 0
        width = new_keys + STEP_OLD
        k = [new_ref[z, 0:NEW, :] for z in range(Z)] if with_new else []
        k += [old_ref[z, at : at + OLD, :] for z in range(Z)]
        v = [new_ref[z, NEW : 2 * NEW, :] for z in range(Z)] if with_new else []
        v += [old_ref[z, at + OLD : at + 2 * OLD, :] for z in range(Z)]
        k, v = jnp.concatenate(k, axis=0), jnp.concatenate(v, axis=0)
        v = jnp.concatenate([v, jnp.ones_like(v)], axis=1)

        def scores(t):
            q = jnp.concatenate(
                [q_ref[:, (t * heads + n) * HEAD : (t * heads + n + 1) * HEAD] for n in range(heads)],
                axis=0,
            )
            s = lax.dot_general(q, k, (((1,), (1,)), ((), ())), preferred_element_type=jnp.float32)
            if masked:
                col = lax.broadcasted_iota(jnp.int32, (tile, width), 1)
                row = lax.broadcasted_iota(jnp.int32, (tile, width), 0) & (NEW - 1)
                new = col < new_keys
                place = jnp.where(new, col + j * STEP_NEW, col - new_keys + j * STEP_OLD)
                limit = jnp.where(new, row + (ctx * NEW + 1), prefix)
                s = jnp.where(place < limit, s, -1e30)
            return s

        s = scores(0)
        for t in range(HEADS // heads):
            ahead = scores(t + 1) if t + 1 < HEADS // heads else None
            r = pl.ds(t * tile, tile)
            old = m_ref[r, :]
            top = jnp.maximum(old, jnp.max(s, axis=1, keepdims=True))
            p = jnp.exp2((s - top[:, :1]) * SCALE)
            factor = jnp.exp2((old - top) * SCALE)
            m_ref[r, :] = top
            pv = jnp.dot(p.astype(jnp.bfloat16), v, preferred_element_type=jnp.float32)
            acc_ref[r, :] = acc_ref[r, :] * jnp.concatenate([factor, factor], axis=1) + pv
            s = ahead

    for i, far in enumerate(apart):
        j = lax.rem(y + far + Y, Y)
        old_full = (j + 1) * STEP_OLD <= prefix
        old_some = j * STEP_OLD < prefix
        if far == 0:
            pl.when(live)(functools.partial(step, i, j, True))
        else:
            pl.when(live & (j < y) & old_full)(functools.partial(step, i, j, False))
            pl.when(live & (j < y) & jnp.logical_not(old_full))(functools.partial(step, i, j, True))
            pl.when(live & (j > y) & old_some)(functools.partial(step, i, j, True, False))

    if last:
        row = lax.broadcasted_iota(jnp.int32, (NEW, HEAD), 0) + ctx * NEW
        for h in range(HEADS):
            a = acc_ref[pl.ds(h * NEW, NEW), :]
            o = a[:, :HEAD] / a[:, HEAD:]
            o_ref[:, h * HEAD : (h + 1) * HEAD] = jnp.where(row < length, o, 0.0).astype(jnp.bfloat16)


def attend(scal, q, blocks, apart, state=None, last=False):
    whole = pl.BlockSpec(memory_space=pltpu.VMEM)
    saved = (
        jax.ShapeDtypeStruct((HEADS * NEW, HEAD), jnp.float32),
        jax.ShapeDtypeStruct((HEADS * NEW, 2 * HEAD), jnp.float32),
    )
    first, count = state is None, len(blocks)
    keys = len(apart) * (STEP_NEW + STEP_OLD)
    return pl.pallas_call(
        functools.partial(attend_kernel, apart=apart, first=first, last=last),
        in_specs=[pl.BlockSpec(memory_space=pltpu.SMEM), whole]
        + [whole] * count
        + ([] if first else [whole] * 2),
        out_specs=whole if last else (whole, whole),
        out_shape=jax.ShapeDtypeStruct((NEW, HEADS * HEAD), jnp.bfloat16) if last else saved,
        input_output_aliases={} if first or last else {2 + count: 0, 3 + count: 1},
        compiler_params=pltpu.CompilerParams(vmem_limit_bytes=24 << 20),
        cost_estimate=pl.CostEstimate(
            flops=COST * HEADS * NEW * keys * HEAD,
            bytes_accessed=len(apart) * Z * ROWS * HEAD * 2,
            transcendentals=HEADS * NEW * keys,
        ),
        name="attend_blocks",
    )(scal, q, *blocks, *(() if first else state))


PAGES = Z * NEW // PAGE


def pick_kernel(scal, pages, *refs):
    blocks, o_ref = refs[:Y], refs[Y]
    y, length = lax.div(scal[0], Z), scal[1]
    row = lax.broadcasted_iota(jnp.int32, (PAGE, HEAD), 0)
    for k in range(o_ref.shape[0]):
        page = pages[k]
        away = lax.rem(lax.div(page, PAGES) - y + Y, Y)
        inside = lax.rem(page, PAGES)
        z = lax.div(inside, NEW // PAGE)
        first = pl.multiple_of(lax.rem(inside, NEW // PAGE) * PAGE, PAGE)
        keep = row < length - page * PAGE
        for half in range(2):
            rows = blocks[0][z, pl.ds(half * NEW + first, PAGE), :]
            for d in range(1, Y):
                rows = jnp.where(away == d, blocks[d][z, pl.ds(half * NEW + first, PAGE), :], rows)
            rows = jnp.where(keep, rows.astype(jnp.float32), 0.0).astype(jnp.bfloat16)
            for core in range(2):
                o_ref[k, core, half * PAGE : (half + 1) * PAGE, :] = rows


def pick(scal, pages, blocks):
    count = pages.shape[0]
    small, whole = pl.BlockSpec(memory_space=pltpu.SMEM), pl.BlockSpec(memory_space=pltpu.VMEM)
    return pl.pallas_call(
        pick_kernel,
        in_specs=[small, small] + [whole] * Y,
        out_specs=whole,
        out_shape=jax.ShapeDtypeStruct((count, 2, 2 * PAGE, HEAD), jnp.bfloat16),
        compiler_params=pltpu.CompilerParams(vmem_limit_bytes=8 << 20),
        name="pick_pages",
    )(scal, pages, *blocks)


def assemble_kernel(core, got_ref, k_ref, v_ref):
    other = 1 - core[0]
    for t in range(got_ref.shape[0]):
        for half, out in enumerate((k_ref, v_ref)):
            out[0, :, t * HEAD : (t + 1) * HEAD] = got_ref[t, other, half * PAGE : (half + 1) * PAGE, :]


def assemble(core, got):
    tps = got.shape[0]
    whole = pl.BlockSpec(memory_space=pltpu.VMEM)
    return pl.pallas_call(
        assemble_kernel,
        in_specs=[pl.BlockSpec(memory_space=pltpu.SMEM), whole],
        out_specs=(whole, whole),
        out_shape=(jax.ShapeDtypeStruct((1, PAGE, tps * HEAD), jnp.bfloat16),) * 2,
        compiler_params=pltpu.CompilerParams(vmem_limit_bytes=8 << 20),
        name="assemble_pages",
    )(core, got)


def body(q, new_k, new_v, old_k, old_v, prompt_len, prefix_len, slots):
    ctx = lax.axis_index(("y", "zh")).astype(jnp.int32)
    core = lax.axis_index("core").astype(jnp.int32)
    tps = lax.axis_size(("x", "zl"))
    scal = jnp.stack([ctx, prompt_len[0], prefix_len[0]])
    mine = jnp.concatenate([new_k[0], new_v[0], old_k[0], old_v[0]], axis=0)
    column = lax.all_gather(mine, "zh", axis=0)
    a, b = [column], [column]
    for _ in range(3):
        a.append(shift(a[-1], ("y",), (-1,), (Y,)))
        b.append(shift(b[-1], ("y",), (1,), (Y,)))
    far = [shift(part, ("y",), (-1,), (Y,)) for part in (a[3][:, : 2 * NEW], a[3][:, 2 * NEW :])]

    slots_here = ctx * tps + jnp.arange(tps, dtype=jnp.int32)
    page_ids = jnp.arange(slots.shape[1], dtype=jnp.int32)
    pages = jnp.sum(jnp.where(slots[0][None, :] == slots_here[:, None], page_ids[None, :], 0), axis=1)
    by_distance = [column, a[1], a[2], a[3], far[0], b[3], b[2], b[1]]
    sent = pick(scal, pages, by_distance).reshape(2 * tps, 2 * PAGE, HEAD)
    got = lax.all_to_all(sent, ("x", "zl", "core"), split_axis=0, concat_axis=0, tiled=True)
    pools = assemble(core[None], got.reshape(tps, 2, 2 * PAGE, HEAD))

    state = attend(scal, q[0], [column], (0,))
    for away in (1, 2, 3):
        state = attend(scal, q[0], [a[away], b[away]], (away, -away), state)
    out = attend(scal, q[0], far, (4,), state, last=True)
    return (out[None], *pools)


def solution(mesh):
    grid = Mesh(mesh.devices.reshape(Y, Z, 4, 2, 2), ("y", "zh", "x", "zl", "core"))
    ctx, tp = ("y", "zh"), ("x", "zl")
    split = P("core", ctx, tp)
    in_specs = (split, split, split, split, split, P("core"), P("core"), P("core", None))
    out_specs = (split, P("core", ctx + tp, None), P("core", ctx + tp, None))
    return jax.shard_map(body, mesh=grid, in_specs=in_specs, out_specs=out_specs, check_vma=False)
```

```python
import functools
import math

import jax
import jax.numpy as jnp
from jax import lax
from jax.experimental import pallas as pl
from jax.experimental.pallas import tpu as pltpu
from jax.sharding import Mesh, PartitionSpec as P

HEAD = 128
PAGE = 16
HEADS = 8
NEW = 128
OLD = 64
ROWS = 2 * NEW + 2 * OLD
Z, Y = 4, 8
STEP_NEW, STEP_OLD = Z * NEW, Z * OLD
COST = 40
SCALE = 1.0 / math.sqrt(HEAD) * math.log2(math.e)


def shift(value, axes, apart, sizes):
    count = math.prod(sizes)

    def moved(i):
        at, out = [], 0
        for size in reversed(sizes):
            at.append(i % size)
            i //= size
        for place, step, size in zip(reversed(at), apart, sizes):
            out = out * size + (place + step) % size
        return out

    return lax.ppermute(value, axes, [(i, moved(i)) for i in range(count)])


def attend_kernel(scal, q_ref, *refs, apart, first, last):
    split = last
    count = len(apart) + split
    blocks, refs = refs[:count], refs[count:]
    if not first:
        m_ref, acc_ref, *refs = refs
    if last:
        (o_ref,) = refs
    else:
        m_ref, acc_ref = refs
    if first:
        m_ref[...] = jnp.full(m_ref.shape, -1e30, jnp.float32)
        acc_ref[...] = jnp.zeros(acc_ref.shape, jnp.float32)
    ctx, length, prefix = scal[0], scal[1], scal[2]
    y = lax.div(ctx, Z)
    live = ctx * NEW < length
    tile = 256
    heads = tile // NEW

    def step(i, j, masked, with_new=True):
        new_ref, old_ref = blocks[i], blocks[-1] if split else blocks[i]
        at = 0 if split else 2 * NEW
        new_keys = STEP_NEW if with_new else 0
        width = new_keys + STEP_OLD
        k = [new_ref[z, 0:NEW, :] for z in range(Z)] if with_new else []
        k += [old_ref[z, at : at + OLD, :] for z in range(Z)]
        v = [new_ref[z, NEW : 2 * NEW, :] for z in range(Z)] if with_new else []
        v += [old_ref[z, at + OLD : at + 2 * OLD, :] for z in range(Z)]
        k, v = jnp.concatenate(k, axis=0), jnp.concatenate(v, axis=0)
        v = jnp.concatenate([v, jnp.ones_like(v)], axis=1)

        def scores(t):
            q = jnp.concatenate(
                [q_ref[:, (t * heads + n) * HEAD : (t * heads + n + 1) * HEAD] for n in range(heads)],
                axis=0,
            )
            s = lax.dot_general(q, k, (((1,), (1,)), ((), ())), preferred_element_type=jnp.float32)
            if masked:
                col = lax.broadcasted_iota(jnp.int32, (tile, width), 1)
                row = lax.broadcasted_iota(jnp.int32, (tile, width), 0) & (NEW - 1)
                new = col < new_keys
                place = jnp.where(new, col + j * STEP_NEW, col - new_keys + j * STEP_OLD)
                limit = jnp.where(new, row + (ctx * NEW + 1), prefix)
                s = jnp.where(place < limit, s, -1e30)
            return s

        s = scores(0)
        for t in range(HEADS // heads):
            ahead = scores(t + 1) if t + 1 < HEADS // heads else None
            r = pl.ds(t * tile, tile)
            old = m_ref[r, :]
            top = jnp.maximum(old, jnp.max(s, axis=1, keepdims=True))
            p = jnp.exp2((s - top[:, :1]) * SCALE)
            factor = jnp.exp2((old - top) * SCALE)
            m_ref[r, :] = top
            pv = jnp.dot(p.astype(jnp.bfloat16), v, preferred_element_type=jnp.float32)
            acc_ref[r, :] = acc_ref[r, :] * jnp.concatenate([factor, factor], axis=1) + pv
            s = ahead

    for i, far in enumerate(apart):
        j = lax.rem(y + far + Y, Y)
        old_full = (j + 1) * STEP_OLD <= prefix
        old_some = j * STEP_OLD < prefix
        if far == 0:
            pl.when(live)(functools.partial(step, i, j, True))
        else:
            pl.when(live & (j < y) & old_full)(functools.partial(step, i, j, False))
            pl.when(live & (j < y) & jnp.logical_not(old_full))(functools.partial(step, i, j, True))
            pl.when(live & (j > y) & old_some)(functools.partial(step, i, j, True, False))

    if last:
        row = lax.broadcasted_iota(jnp.int32, (NEW, HEAD), 0) + ctx * NEW
        for h in range(HEADS):
            a = acc_ref[pl.ds(h * NEW, NEW), :]
            o = a[:, :HEAD] / a[:, HEAD:]
            o_ref[:, h * HEAD : (h + 1) * HEAD] = jnp.where(row < length, o, 0.0).astype(jnp.bfloat16)


def attend(scal, q, blocks, apart, state=None, last=False):
    whole = pl.BlockSpec(memory_space=pltpu.VMEM)
    saved = (
        jax.ShapeDtypeStruct((HEADS * NEW, HEAD), jnp.float32),
        jax.ShapeDtypeStruct((HEADS * NEW, 2 * HEAD), jnp.float32),
    )
    first, count = state is None, len(blocks)
    keys = len(apart) * (STEP_NEW + STEP_OLD)
    return pl.pallas_call(
        functools.partial(attend_kernel, apart=apart, first=first, last=last),
        in_specs=[pl.BlockSpec(memory_space=pltpu.SMEM), whole]
        + [whole] * count
        + ([] if first else [whole] * 2),
        out_specs=whole if last else (whole, whole),
        out_shape=jax.ShapeDtypeStruct((NEW, HEADS * HEAD), jnp.bfloat16) if last else saved,
        input_output_aliases={} if first or last else {2 + count: 0, 3 + count: 1},
        compiler_params=pltpu.CompilerParams(vmem_limit_bytes=24 << 20),
        cost_estimate=pl.CostEstimate(
            flops=COST * HEADS * NEW * keys * HEAD,
            bytes_accessed=len(apart) * Z * ROWS * HEAD * 2,
            transcendentals=HEADS * NEW * keys,
        ),
        name="attend_blocks",
    )(scal, q, *blocks, *(() if first else state))


PAGES = Z * NEW // PAGE


def pick_kernel(scal, pages, *refs):
    blocks, o_ref = refs[:Y], refs[Y]
    y, length = lax.div(scal[0], Z), scal[1]
    row = lax.broadcasted_iota(jnp.int32, (PAGE, HEAD), 0)
    for k in range(o_ref.shape[1]):
        page = pages[k]
        away = lax.rem(lax.div(page, PAGES) - y + Y, Y)
        inside = lax.rem(page, PAGES)
        z = lax.div(inside, NEW // PAGE)
        first = pl.multiple_of(lax.rem(inside, NEW // PAGE) * PAGE, PAGE)
        keep = row < length - page * PAGE
        for half in range(2):
            rows = blocks[0][z, pl.ds(half * NEW + first, PAGE), :]
            for d in range(1, Y):
                rows = jnp.where(away == d, blocks[d][z, pl.ds(half * NEW + first, PAGE), :], rows)
            rows = jnp.where(keep, rows.astype(jnp.float32), 0.0).astype(jnp.bfloat16)
            for core in range(2):
                o_ref[core, k, half * PAGE : (half + 1) * PAGE, :] = rows


def pick(scal, pages, blocks):
    count = pages.shape[0]
    small, whole = pl.BlockSpec(memory_space=pltpu.SMEM), pl.BlockSpec(memory_space=pltpu.VMEM)
    return pl.pallas_call(
        pick_kernel,
        in_specs=[small, small] + [whole] * Y,
        out_specs=whole,
        out_shape=jax.ShapeDtypeStruct((2, count, 2 * PAGE, HEAD), jnp.bfloat16),
        compiler_params=pltpu.CompilerParams(vmem_limit_bytes=8 << 20),
        name="pick_pages",
    )(scal, pages, *blocks)


def assemble_kernel(core, got_ref, k_ref, v_ref):
    other = 1 - core[0]
    for t in range(got_ref.shape[1]):
        for half, out in enumerate((k_ref, v_ref)):
            out[0, :, t * HEAD : (t + 1) * HEAD] = got_ref[other, t, half * PAGE : (half + 1) * PAGE, :]


def assemble(core, got):
    tps = got.shape[1]
    whole = pl.BlockSpec(memory_space=pltpu.VMEM)
    return pl.pallas_call(
        assemble_kernel,
        in_specs=[pl.BlockSpec(memory_space=pltpu.SMEM), whole],
        out_specs=(whole, whole),
        out_shape=(jax.ShapeDtypeStruct((1, PAGE, tps * HEAD), jnp.bfloat16),) * 2,
        compiler_params=pltpu.CompilerParams(vmem_limit_bytes=8 << 20),
        name="assemble_pages",
    )(core, got)


def body(q, new_k, new_v, old_k, old_v, prompt_len, prefix_len, slots):
    ctx = lax.axis_index(("y", "zh")).astype(jnp.int32)
    core = lax.axis_index("core").astype(jnp.int32)
    tps = lax.axis_size(("x", "zl"))
    scal = jnp.stack([ctx, prompt_len[0], prefix_len[0]])
    mine = jnp.concatenate([new_k[0], new_v[0], old_k[0], old_v[0]], axis=0)
    column = lax.all_gather(mine, "zh", axis=0)
    a, b = [column], [column]
    for _ in range(3):
        a.append(shift(a[-1], ("y",), (-1,), (Y,)))
        b.append(shift(b[-1], ("y",), (1,), (Y,)))
    far = [shift(part, ("y",), (-1,), (Y,)) for part in (a[3][:, : 2 * NEW], a[3][:, 2 * NEW :])]

    slots_here = ctx * tps + jnp.arange(tps, dtype=jnp.int32)
    page_ids = jnp.arange(slots.shape[1], dtype=jnp.int32)
    pages = jnp.sum(jnp.where(slots[0][None, :] == slots_here[:, None], page_ids[None, :], 0), axis=1)
    by_distance = [column, a[1], a[2], a[3], far[0], b[3], b[2], b[1]]
    sent = pick(scal, pages, by_distance).reshape(2 * tps, 2 * PAGE, HEAD)
    got = lax.all_to_all(sent, ("core", "x", "zl"), split_axis=0, concat_axis=0, tiled=True)
    pools = assemble(core[None], got.reshape(2, tps, 2 * PAGE, HEAD))

    state = attend(scal, q[0], [column], (0,))
    for away in (1, 2, 3):
        state = attend(scal, q[0], [a[away], b[away]], (away, -away), state)
    out = attend(scal, q[0], far, (4,), state, last=True)
    return (out[None], *pools)


def solution(mesh):
    grid = Mesh(mesh.devices.reshape(Y, Z, 4, 2, 2), ("y", "zh", "x", "zl", "core"))
    ctx, tp = ("y", "zh"), ("x", "zl")
    split = P("core", ctx, tp)
    in_specs = (split, split, split, split, split, P("core"), P("core"), P("core", None))
    out_specs = (split, P("core", ctx + tp, None), P("core", ctx + tp, None))
    return jax.shard_map(body, mesh=grid, in_specs=in_specs, out_specs=out_specs, check_vma=False)
```
